256 devices in a mesh: seq: 64 (over x, z, core), head: 4 (over y).
Axes of the slice: x: 4, y: 4, z: 8, core: 2. Of those that a mesh axis runs over, the one named last changes fastest.
Arguments:
- att_q: bfloat16 [8192, 2048], P('seq', 'head'), may hold values from -120 to 120
- att_k: bfloat16 [8192, 2048], P('seq', 'head'), may hold values from -4 to 4
- att_v: bfloat16 [8192, 2048], P('seq', 'head'), may hold values from -6 to 6
- att_dy: bfloat16 [8192, 2048], P('seq', 'head'), may hold values from -6 to 6
- att_out_w: bfloat16 [2048, 2048], P('head'), may hold values from -0.125 to 0.125
- gdn_q: bfloat16 [8192, 2048], P('seq', 'head'), may hold values from -0.5 to 0.5
- gdn_k: bfloat16 [8192, 2048], P('seq', 'head'), may hold values from -1 to 1, as said below
- gdn_v: bfloat16 [8192, 2048], P('seq', 'head'), may hold values from -6 to 6
- gdn_beta: float32 [16, 8192], P('head', 'seq'), may hold values from 0.001 to 0.95
- gdn_gate: float32 [16, 8192], P('head', 'seq'), may hold values from -3 to 0
- gdn_state: float32 [64, 16, 128, 128], P('seq', 'head'), may hold values from -1.5 to 1.5
- gdn_dy: bfloat16 [8192, 2048], P('seq', 'head'), may hold values from -3 to 3
- gdn_out_w: bfloat16 [2048, 2048], P('head'), may hold values from -0.125 to 0.125
Outputs:
- att_dq: bfloat16 [8192, 2048], P('seq', 'head')
- att_dk: bfloat16 [8192, 2048], P('seq', 'head')
- att_dv: bfloat16 [8192, 2048], P('seq', 'head')
- gdn_dq: bfloat16 [8192, 2048], P('seq', 'head')
- gdn_dk: bfloat16 [8192, 2048], P('seq', 'head')
- gdn_dv: bfloat16 [8192, 2048], P('seq', 'head')
- gdn_dbeta: float32 [16, 8192], P('head', 'seq')
- gdn_dgate: float32 [16, 8192], P('head', 'seq')
The draws below stay inside these ranges and needn't reach their ends.
Inputs may be any that keep to these rules, and one draw needn't show every extreme that they name: `gdn_k`: the 128 features of one head for one token form a vector of length one, up to rounding.
All inputs are finite; a program needn't handle non-finite values.
Results may differ from the reference program's by a relative error of at most 0.014.
Values may be sent and summed in bfloat16 or wider, within the bound.
No kernel may reach another device: no remote copies, remote signals or barrier semaphores. Data moves between devices by JAX's collectives and lax.ppermute only.
A program may use at most 192 MiB of HBM per device.

```python
import math
import jax
import jax.numpy as jnp
from jax import lax

D = 2048
HEADS = 16
HD = 128
WINDOW = 1024
GROUP = 64
DOCS = 2
TOK_DEV = 128
TOKENS = 8192
BLOCKS = 64


def attention_draws(key):
    width = HEADS * HD
    key_vals = jnp.clip(jax.random.normal(jax.random.fold_in(key, 11), (TOKENS, width), jnp.float32), -4.0, 4.0)
    queries = jnp.clip(jax.random.normal(jax.random.fold_in(key, 12), (TOKENS, width), jnp.float32), -4.0, 4.0)
    return (queries, key_vals)


def draw_att_q(key, part):
    return attention_draws(key)[0].astype(jnp.bfloat16)


def draw_att_k(key, part):
    return attention_draws(key)[1].astype(jnp.bfloat16)


def slow_heads(key):
    order = jax.random.permutation(jax.random.fold_in(key, 31), HEADS)
    count = HEADS // 2
    return (order < count)[:, None]


def draw_gdn_k(key, part):
    raw = jnp.clip(jax.random.normal(jax.random.fold_in(key, 51), (TOKENS, HEADS, HD), jnp.float32), -4.0, 4.0)
    raw = jnp.where(jnp.abs(raw) < 0.001, 0.001, raw)
    length = jnp.sqrt(jnp.sum(raw * raw, axis=2, keepdims=True))
    return (raw / length).reshape(TOKENS, HEADS * HD).astype(jnp.bfloat16)


def draw_gdn_beta(key, part):
    slow_pick = slow_heads(key)
    slow_beta = jnp.exp(jax.random.uniform(jax.random.fold_in(key, 41), (HEADS, TOKENS), jnp.float32, math.log(0.001), math.log(0.02)))
    fast_beta = jax.nn.sigmoid(jnp.clip(jax.random.normal(jax.random.fold_in(key, 42), (HEADS, TOKENS), jnp.float32), -2.9, 2.9))
    return jnp.where(slow_pick, slow_beta, fast_beta).astype(jnp.float32)


def draw_gdn_gate(key, part):
    slow_pick = slow_heads(key)
    slow_rate = jnp.exp(jax.random.uniform(jax.random.fold_in(key, 22), (HEADS, 1), jnp.float32, math.log(2e-06), math.log(1e-05)))
    fast_rate = jnp.exp(jax.random.uniform(jax.random.fold_in(key, 23), (HEADS, 1), jnp.float32, math.log(1.0 / 50.0), math.log(1.0 / 30.0)))
    base_rate = jnp.where(slow_pick, slow_rate, fast_rate)
    token_factor = jnp.exp(jax.random.uniform(jax.random.fold_in(key, 24), (HEADS, TOKENS), jnp.float32, -math.log(2.0), math.log(2.0)))
    block_factor = jnp.exp(jax.random.uniform(jax.random.fold_in(key, 25), (1, TOKENS // TOK_DEV), jnp.float32, -math.log(2.0), math.log(2.0)))
    block_factor = jnp.repeat(block_factor, TOK_DEV, axis=1)
    gate_log = -base_rate * token_factor * block_factor
    spots = jax.random.randint(jax.random.fold_in(key, 26), (2 * DOCS,), 0, TOKENS)
    depth = jax.random.uniform(jax.random.fold_in(key, 27), (2 * DOCS,), jnp.float32, math.log(0.5), math.log(0.8))
    hits = jnp.arange(TOKENS)[None, :] == spots[:, None]
    gate_log = gate_log + jnp.sum(jnp.where(hits, depth[:, None], 0.0), axis=0)[None, :]
    return gate_log.astype(jnp.float32)


def shard_levels(own_key, extent, split, low, high):
    def one(position, blocks):
        draws = jax.random.uniform(jax.random.fold_in(jax.random.fold_in(own_key, 6), position), (blocks,), jnp.float32, low / len(split), high / len(split))
        return jnp.repeat(jnp.exp(draws), extent[position] // blocks).reshape((-1,) + (1,) * (len(extent) - position - 1))

    gain = one(*split[0])
    for cut in split[1:]:
        gain = gain * one(*cut)
    return gain


def noise(own_key, extent, scale, most, cuts=(), kind=jnp.bfloat16):
    values = scale * jax.random.normal(own_key, extent, jnp.float32)
    if cuts:
        values = values * shard_levels(own_key, extent, cuts, -0.22, 0.18)
    return jnp.clip(values, -most, most).astype(kind)


def setup_inputs(seed: int = 0) -> dict:
    seeds = jax.random.split(jax.random.key(seed), 14)
    att_q = draw_att_q(jax.random.fold_in(seeds[13], 71), 0)
    att_k = draw_att_k(jax.random.fold_in(seeds[13], 71), 0)
    att_v = noise(seeds[2], (TOKENS, HEADS * HD), 1.0, 6.0, ((0, 64), (1, 4)))
    att_dy = noise(seeds[3], (TOKENS, D), 1.0, 6.0, ((0, 64), (1, 4)))
    att_out_w = noise(seeds[4], (HEADS * HD, D), D ** -0.5, 0.125, ((0, 4),))
    gdn_q = noise(seeds[5], (TOKENS, HEADS * HD), HD ** -0.5, 0.5, ((0, 64), (1, 4)))
    gdn_k = draw_gdn_k(jax.random.fold_in(seeds[13], 71), 0)
    gdn_v = noise(seeds[7], (TOKENS, HEADS * HD), 1.0, 6.0, ((0, 64), (1, 4)))
    gdn_beta = draw_gdn_beta(jax.random.fold_in(seeds[13], 71), 0)
    gdn_gate = draw_gdn_gate(jax.random.fold_in(seeds[13], 71), 0)
    gdn_state = noise(seeds[10], (BLOCKS, HEADS, HD, HD), 0.1, 1.5, ((0, 64), (1, 4)), jnp.float32)
    gdn_dy = noise(seeds[11], (TOKENS, D), 0.2, 3.0, ((0, 64), (1, 4)))
    gdn_out_w = noise(seeds[12], (HEADS * HD, D), D ** -0.5, 0.125, ((0, 4),))
    return {"att_q": att_q, "att_k": att_k, "att_v": att_v, "att_dy": att_dy, "att_out_w": att_out_w, "gdn_q": gdn_q, "gdn_k": gdn_k, "gdn_v": gdn_v, "gdn_beta": gdn_beta, "gdn_gate": gdn_gate, "gdn_state": gdn_state, "gdn_dy": gdn_dy, "gdn_out_w": gdn_out_w}


def exact_dot(left, right):
    return jnp.dot(left, right, precision=lax.Precision.HIGHEST)

def group_terms(key_rows, beta_rates, gate_log):
    size_c = key_rows.shape[0]
    cum_log = jnp.cumsum(gate_log)
    growth = jnp.exp(cum_log)
    row_ids = jnp.arange(size_c)[:, None]
    col_ids = jnp.arange(size_c)[None, :]
    decays = jnp.where(row_ids >= col_ids, jnp.exp(jnp.minimum(cum_log[:, None] - cum_log[None, :], 0.0)), 0.0)
    key_gram = exact_dot(key_rows, key_rows.T)
    system = jnp.eye(size_c, dtype=jnp.float32) + jnp.where(row_ids > col_ids, beta_rates[:, None] * decays * key_gram, 0.0)
    return (cum_log, growth, decays, system)

def group_step(carried, pieces):
    queries, key_rows, values, beta_rates, gate_log = pieces
    head_dim = key_rows.shape[1]
    cum_log, growth, decays, system = group_terms(key_rows, beta_rates, gate_log)
    right_side = beta_rates[:, None] * jnp.concatenate([values, growth[:, None] * key_rows], axis=1)
    solved = lax.linalg.triangular_solve(system, right_side, left_side=True, lower=True, unit_diagonal=True)
    upd_vals = solved[:, :head_dim]
    wy_keys = solved[:, head_dim:]
    fresh_vals = upd_vals - exact_dot(wy_keys, carried.T)
    outputs = growth[:, None] * exact_dot(queries, carried.T) + exact_dot(exact_dot(queries, key_rows.T) * decays, fresh_vals)
    tail_decay = jnp.exp(cum_log[-1] - cum_log)
    carried = growth[-1] * carried + exact_dot((fresh_vals * tail_decay[:, None]).T, key_rows)
    return (carried, outputs)

def head_forward(queries, key_rows, values, beta_rates, gate_log, carried):
    count = queries.shape[0] // GROUP

    def into_groups(array):
        return array.reshape((count, GROUP) + array.shape[1:])
    carried, outputs = lax.scan(group_step, carried, (into_groups(queries), into_groups(key_rows), into_groups(values), into_groups(beta_rates), into_groups(gate_log)))
    return (outputs.reshape(queries.shape), carried)

def block_forward(queries, key_rows, values, beta_rates, gate_log, carried):
    token_count, width = queries.shape
    head_count = carried.shape[0]

    def split_heads(array):
        return array.reshape(token_count, head_count, HD).transpose(1, 0, 2)
    outputs, carried = jax.vmap(head_forward)(split_heads(queries), split_heads(key_rows), split_heads(values), beta_rates, gate_log, carried)
    return (outputs.transpose(1, 0, 2).reshape(token_count, width), carried)

def window_backward(queries, key_rows, values, dout, query_pos, key_pos, doc_len):
    q_count, width = queries.shape
    k_count = key_rows.shape[0]
    heads_here = width // HD
    scale = 1.0 / math.sqrt(HD)
    q_heads = queries.astype(jnp.float32).reshape(q_count, heads_here, HD)
    k_heads = key_rows.astype(jnp.float32).reshape(k_count, heads_here, HD)
    v_heads = values.astype(jnp.float32).reshape(k_count, heads_here, HD)
    d_heads = dout.astype(jnp.float32).reshape(q_count, heads_here, HD)
    scores = jnp.einsum('qhd,khd->hqk', q_heads, k_heads) * scale
    doc_start = query_pos // doc_len * doc_len
    visible = (key_pos[None, :] <= query_pos[:, None]) & (key_pos[None, :] > query_pos[:, None] - WINDOW) & (key_pos[None, :] >= doc_start[:, None])
    scores = jnp.where(visible[None], scores, -jnp.inf)
    row_max = lax.optimization_barrier(jnp.max(scores, axis=2, keepdims=True))
    expo = jnp.exp(scores - row_max)
    weights = expo / lax.optimization_barrier(jnp.sum(expo, axis=2, keepdims=True))
    weights_bf = lax.optimization_barrier(weights.astype(jnp.bfloat16)).astype(jnp.float32)
    dweights = jnp.einsum('qhd,khd->hqk', d_heads, v_heads)
    row_dots = lax.optimization_barrier(jnp.sum(weights * dweights, axis=2, keepdims=True))
    dscore_bf = lax.optimization_barrier((weights * (dweights - row_dots)).astype(jnp.bfloat16)).astype(jnp.float32)
    grad_q = jnp.einsum('hqk,khd->qhd', dscore_bf, k_heads) * scale
    grad_k = jnp.einsum('hqk,qhd->khd', dscore_bf, q_heads) * scale
    grad_v = jnp.einsum('hqk,qhd->khd', weights_bf, d_heads)
    return (grad_q.reshape(q_count, width), grad_k.reshape(k_count, width), grad_v.reshape(k_count, width))

def reference(att_q, att_k, att_v, att_dy, att_out_w, gdn_q, gdn_k, gdn_v, gdn_beta, gdn_gate, gdn_state, gdn_dy, gdn_out_w):
    att_dout = jnp.dot(att_dy.astype(jnp.float32), att_out_w.T.astype(jnp.float32), preferred_element_type=jnp.float32).astype(jnp.bfloat16)
    gdn_dout = jnp.dot(gdn_dy.astype(jnp.float32), gdn_out_w.T.astype(jnp.float32), preferred_element_type=jnp.float32).astype(jnp.bfloat16)
    reach = WINDOW // TOK_DEV
    margin = reach * TOK_DEV
    doc_len = TOKENS // DOCS
    per_doc = BLOCKS // DOCS
    width = HEADS * HD
    pad_k = jnp.concatenate([jnp.zeros((margin, width), jnp.bfloat16), att_k], axis=0)
    pad_v = jnp.concatenate([jnp.zeros((margin, width), jnp.bfloat16), att_v], axis=0)
    block_ids = jnp.arange(BLOCKS, dtype=jnp.int32)

    def att_block(totals, block_id):
        start = (block_id * TOK_DEV).astype(jnp.int32)
        q_rows = lax.dynamic_slice_in_dim(att_q, start, TOK_DEV, 0)
        d_rows = lax.dynamic_slice_in_dim(att_dout, start, TOK_DEV, 0)
        k_rows = lax.dynamic_slice_in_dim(pad_k, start, margin + TOK_DEV, 0)
        v_rows = lax.dynamic_slice_in_dim(pad_v, start, margin + TOK_DEV, 0)
        query_pos = start + jnp.arange(TOK_DEV, dtype=jnp.int32)
        key_pos = start - margin + jnp.arange(margin + TOK_DEV, dtype=jnp.int32)
        grad_q, grad_k, grad_v = window_backward(q_rows, k_rows, v_rows, d_rows, query_pos, key_pos, doc_len)
        acc_k, acc_v = totals
        acc_k = lax.dynamic_update_slice_in_dim(acc_k, lax.dynamic_slice_in_dim(acc_k, start, margin + TOK_DEV, 0) + grad_k, start, 0)
        acc_v = lax.dynamic_update_slice_in_dim(acc_v, lax.dynamic_slice_in_dim(acc_v, start, margin + TOK_DEV, 0) + grad_v, start, 0)
        return ((acc_k, acc_v), grad_q.astype(jnp.bfloat16))
    empty = jnp.zeros((margin + TOKENS, width), jnp.float32)
    (acc_k, acc_v), grad_q_blocks = lax.scan(att_block, (empty, empty), block_ids)
    att_dq = grad_q_blocks.reshape(TOKENS, width)
    att_dk = acc_k[margin:].astype(jnp.bfloat16)
    att_dv = acc_v[margin:].astype(jnp.bfloat16)

    def gdn_block(adjoint, block_id):
        start = (block_id * TOK_DEV).astype(jnp.int32)
        q_rows = lax.dynamic_slice_in_dim(gdn_q, start, TOK_DEV, 0).astype(jnp.float32)
        k_rows = lax.dynamic_slice_in_dim(gdn_k, start, TOK_DEV, 0).astype(jnp.float32)
        v_rows = lax.dynamic_slice_in_dim(gdn_v, start, TOK_DEV, 0).astype(jnp.float32)
        d_rows = lax.dynamic_slice_in_dim(gdn_dout, start, TOK_DEV, 0).astype(jnp.float32)
        beta_rows = lax.dynamic_slice_in_dim(gdn_beta, start, TOK_DEV, 1)
        gate_rows = lax.dynamic_slice_in_dim(gdn_gate, start, TOK_DEV, 1)
        start_state = lax.dynamic_index_in_dim(gdn_state, block_id, 0, keepdims=False)
        forward_out, pull_back = jax.vjp(block_forward, q_rows, k_rows, v_rows, beta_rows, gate_rows, start_state)
        grads = pull_back((d_rows, adjoint))
        keep_flag = (block_id % per_doc != 0).astype(jnp.float32)
        return (grads[5] * keep_flag, (grads[0].astype(jnp.bfloat16), grads[1].astype(jnp.bfloat16), grads[2].astype(jnp.bfloat16), grads[3], grads[4]))
    _, gathered = lax.scan(gdn_block, jnp.zeros((HEADS, HD, HD), jnp.float32), block_ids, reverse=True)
    gdn_dq = gathered[0].reshape(TOKENS, width)
    gdn_dk = gathered[1].reshape(TOKENS, width)
    gdn_dv = gathered[2].reshape(TOKENS, width)
    gdn_dbeta = gathered[3].transpose(1, 0, 2).reshape(HEADS, TOKENS)
    gdn_dgate = gathered[4].transpose(1, 0, 2).reshape(HEADS, TOKENS)
    return (att_dq, att_dk, att_dv, gdn_dq, gdn_dk, gdn_dv, gdn_dbeta, gdn_dgate)
```

```python
import math

import jax
import jax.numpy as jnp
from jax import lax
from jax.experimental import pallas as pl
from jax.experimental.pallas import tpu as pltpu
from jax.sharding import PartitionSpec as P

HD = 128
PAIR = 256
RING = 4
SEG = 4
SEGS = 8
DOCS = 2
F32 = jnp.float32
BF16 = jnp.bfloat16
NN = (((1,), (0,)), ((), ()))
NT = (((1,), (1,)), ((), ()))
TN = (((0,), (0,)), ((), ()))
FAR = -1e30


def dot(left, right, dims):
    return lax.dot_general(left, right, dims, preferred_element_type=F32)


def exact(left, right, dims):
    return lax.dot_general(
        left, right, dims, precision=lax.Precision.HIGHEST, preferred_element_type=F32
    )


def split(value):
    high = value.astype(BF16)
    return high, (value - high.astype(F32)).astype(BF16)


def dot_l(left, right, dims):
    high, low = split(left)
    return dot(high, right, dims) + dot(low, right, dims)


def dot_r(left, right, dims):
    high, low = split(right)
    return dot(left, high, dims) + dot(left, low, dims)


def dot3(left, right, dims):
    lh, ll = split(left)
    rh, rl = split(right)
    return dot(lh, rh, dims) + (dot(lh, rl, dims) + dot(ll, rh, dims))


def grid_ids(rows, cols):
    return (
        lax.broadcasted_iota(jnp.int32, (rows, cols), 0),
        lax.broadcasted_iota(jnp.int32, (rows, cols), 1),
    )


def head_cols(head):
    return slice(head * HD, (head + 1) * HD)


def token_rates(beta, gate, heads):
    rows, cols = grid_ids(HD, HD)
    pad = jnp.zeros((8 - heads, HD), F32)
    beta8 = jnp.concatenate([beta, pad])
    gate8 = jnp.concatenate([gate, pad])
    upto = (rows <= cols).astype(F32)
    crow = exact(gate8, upto, NN)
    ccol = exact((cols <= rows).astype(F32), gate8, NT)
    bcol = exact((cols == rows).astype(F32), beta8, NT)
    return crow, ccol, bcol, beta8


def gdn_pre_body(q_ref, k_ref, beta_ref, gate_ref, m_ref, n_ref, delta_ref, *, heads):
    rows, cols = grid_ids(HD, HD)
    crow, ccol, bcol, brow = token_rates(beta_ref[...], gate_ref[...], heads)
    lower = rows >= cols
    strict = rows > cols
    eye = (rows == cols).astype(F32)
    systems = []
    mixes = []
    for h in range(heads):
        k = k_ref[:, head_cols(h)]
        q = q_ref[:, head_cols(h)]
        decay = jnp.exp(jnp.minimum(ccol[:, h : h + 1] - crow[h : h + 1, :], 0.0))
        systems.append(jnp.where(strict, bcol[:, h : h + 1] * decay * dot(k, k, NT), 0.0))
        mixes.append(jnp.where(lower, decay * dot(q, k, NT), 0.0))
    pair = (rows >> 1) == (cols >> 1)
    inverse = [eye - jnp.where(pair, s, 0.0) for s in systems]
    for level in range(1, 7):
        ring = ((rows >> (level + 1)) == (cols >> (level + 1))) & ((rows >> level) != (cols >> level))
        part = [dot3(m, jnp.where(ring, s, 0.0), NN) for m, s in zip(inverse, systems)]
        inverse = [m - dot3(x, m, NN) for m, x in zip(inverse, part)]
    for h in range(heads):
        k = k_ref[:, head_cols(h)]
        q = q_ref[:, head_cols(h)]
        last = crow[h : h + 1, HD - 1 :]
        grow = jnp.exp(crow[h : h + 1, :])
        gcol = jnp.exp(ccol[:, h : h + 1])
        tcol = jnp.exp(jnp.minimum(last - ccol[:, h : h + 1], 0.0))
        wy = dot_l(inverse[h] * (brow[h : h + 1, :] * grow), k, NN)
        m_ref[h] = inverse[h]
        n_ref[h] = gcol * q.astype(F32) - dot3(mixes[h], wy, NN)
        delta_ref[h, :HD, :] = dot_r(k, tcol * wy, TN).astype(BF16)
        total = jnp.broadcast_to(jnp.exp(last), (16, HD))
        high = total.astype(BF16).astype(F32)
        mid = (total - high).astype(BF16).astype(F32)
        low = total - high - mid
        tile_row = lax.broadcasted_iota(jnp.int32, (16, HD), 0)
        tile = jnp.where(
            tile_row == 0, high, jnp.where(tile_row == 1, mid, jnp.where(tile_row == 2, low, 0.0))
        )
        delta_ref[h, HD:, :] = tile.astype(BF16)


def project(parts, w_ref, owners, width):
    total = None
    for part, owner in zip(parts, owners):
        span = pl.ds(pl.multiple_of(owner * width, width), width)
        term = dot(part[...], w_ref[:, span], NT)
        total = term if total is None else total + term
    return total.astype(BF16)


def shard_owners():
    own = lax.axis_index("head")
    count = lax.axis_size("head")
    return [(own - shift + count) % count for shift in range(count)]


def gdn_dout_body(d0, d1, d2, d3, w_ref, n_ref, delta_ref, dout_ref, send_ref, *, heads):
    dout = project((d0, d1, d2, d3), w_ref, shard_owners(), d0.shape[1])
    dout_ref[...] = dout
    for h in range(heads):
        send_ref[h, : HD + 16, :] = delta_ref[h]
        send_ref[h, HD + 16 :, :] = dot_r(dout[:, head_cols(h)], n_ref[h], TN).astype(BF16)


def unpack_map(payload):
    delta = payload[:HD]
    tile = payload[HD : HD + 16].astype(F32)
    gain = tile[0:1] + tile[1:2] + tile[2:3]
    return gain, delta, payload[HD + 16 :].astype(F32)


def chain_fold_body(blocks_ref, out_ref):
    gain, delta, local = unpack_map(blocks_ref[SEG - 1])
    both = jnp.concatenate([delta.astype(F32), local])
    for b in range(SEG - 2, -1, -1):
        next_gain, next_delta, next_local = unpack_map(blocks_ref[b])
        moved = next_gain * both - dot_l(both, next_delta, NN)
        both = moved + jnp.concatenate([gain * next_delta.astype(F32), next_local])
        gain = gain * next_gain
    out_ref[:HD, :] = both[:HD].astype(BF16)
    out_ref[HD + 16 :, :] = both[HD:].astype(BF16)
    total = jnp.broadcast_to(gain, (16, HD))
    high = total.astype(BF16).astype(F32)
    mid = (total - high).astype(BF16).astype(F32)
    low = total - high - mid
    tile_row = lax.broadcasted_iota(jnp.int32, (16, HD), 0)
    tile = jnp.where(
        tile_row == 0, high, jnp.where(tile_row == 1, mid, jnp.where(tile_row == 2, low, 0.0))
    )
    out_ref[HD : HD + 16, :] = tile.astype(BF16)


def chain_walk_body(*refs):
    later, blocks_ref, out_ref = refs[: SEGS - 1], refs[SEGS - 1], refs[SEGS]
    adjoint = jnp.zeros((HD, HD), F32)

    def step(adjoint, payload):
        gain, delta, local = unpack_map(payload)
        high, low = split(adjoint)
        both = dot(jnp.concatenate([high, low]), delta, NN)
        return gain * adjoint - (both[:HD] + both[HD:]) + local

    for seg in range(SEGS - 2, -1, -1):
        adjoint = step(adjoint, later[seg][...])
    for b in range(SEG - 1, -1, -1):
        out_ref[b] = adjoint.astype(BF16)
        if b:
            adjoint = step(adjoint, blocks_ref[b])


def gdn_post_body(
    q_ref, k_ref, v_ref, beta_ref, gate_ref, s_ref, m_ref, dout_ref, a_ref,
    dq_ref, dk_ref, dv_ref, dbeta_ref, dgate_ref, *, heads,
):
    rows, cols = grid_ids(HD, HD)
    crow, ccol, bcol, _ = token_rates(beta_ref[...], gate_ref[...], heads)
    lower = rows >= cols
    strict = rows > cols
    after = jnp.zeros((HD, HD), F32)
    before = jnp.zeros((HD, HD), F32)
    rates = jnp.zeros((HD, HD), F32)
    row8 = lax.broadcasted_iota(jnp.int32, (8, HD), 0)
    taken = jnp.zeros((8, HD), F32)
    whole = jnp.zeros((8, HD), F32)
    for h in range(heads):
        q = q_ref[:, head_cols(h)]
        k = k_ref[:, head_cols(h)]
        v = v_ref[:, head_cols(h)].astype(F32)
        dout = dout_ref[:, head_cols(h)]
        state = s_ref[h]
        inverse = m_ref[h]
        adjoint = a_ref[h]
        b = bcol[:, h : h + 1]
        c = ccol[:, h : h + 1]
        last = crow[h : h + 1, HD - 1 :]
        g = jnp.exp(c)
        t = jnp.exp(jnp.minimum(last - c, 0.0))
        decay = jnp.where(lower, jnp.exp(jnp.minimum(c - crow[h : h + 1, :], 0.0)), 0.0)
        gram = decay * dot(k, k, NT)
        mix = decay * dot(q, k, NT)
        k_s = dot_r(k, state, NT)
        q_s = dot_r(q, state, NT)
        resid = v - g * k_s
        fresh = dot3(inverse, b * resid, NN)
        k_a = dot(k, adjoint, NT)
        dfresh = dot_l(mix, dout, TN) + t * k_a
        dright = dot3(inverse, dfresh, TN)
        dmix = dot_r(dout, fresh, NT)
        dsys = jnp.where(strict, -dot3(dright, fresh, NT), 0.0)
        x_mix = dmix * decay
        x_sys = dsys * (b * decay)
        dq_ref[:, head_cols(h)] = (g * dot_r(dout, state, NN) + dot_l(x_mix, k, NN)).astype(BF16)
        dk = dot_l(x_mix, q, TN) + dot_l(x_sys, k, NN) + dot_l(x_sys, k, TN)
        dk = dk + dot_l(t * fresh, adjoint, NN) - dot3((b * g) * dright, state, NN)
        dk_ref[:, head_cols(h)] = dk.astype(BF16)
        dv_ref[:, head_cols(h)] = (b * dright).astype(BF16)
        dbeta = jnp.sum(dright * resid + dsys * gram, axis=1, keepdims=True)
        flow = dmix * mix + dsys * (b * gram)
        dgrow = jnp.sum(
            g * (dout.astype(F32) * q_s - b * dright * k_s) + flow, axis=1, keepdims=True
        )
        dtail = jnp.sum(t * fresh * k_a, axis=1, keepdims=True)
        ends = jnp.exp(last) * jnp.sum(
            jnp.sum(adjoint.astype(F32) * state, axis=1, keepdims=True), axis=0, keepdims=True
        )
        after = jnp.where(cols == h, dgrow, after)
        before = jnp.where(cols == h, dtail, before)
        rates = jnp.where(cols == h, dbeta, rates)
        taken = jnp.where(row8 == h, jnp.sum(flow, axis=0, keepdims=True), taken)
        whole = jnp.where(row8 == h, ends, whole)
    not_before = (rows >= cols).astype(F32)
    dgate = exact(after, not_before, TN) + exact(before, (rows < cols).astype(F32), TN)
    dgate = dgate[:8] + whole - exact(taken, not_before, NN)
    dgate_ref[...] = dgate[:heads]
    dbeta_ref[...] = exact(rates, (rows == cols).astype(F32), TN)[:heads]


def core_side():
    return lax.axis_index("seq") % 2


def half(side):
    return slice(side * PAIR, (side + 1) * PAIR)


def pack_body(q_ref, k_ref, v_ref, send_ref):
    side = core_side()
    for own in range(2):

        @pl.when(side == own)
        def _():
            for i, ref in enumerate((q_ref, k_ref, v_ref)):
                send_ref[i] = ref[:, half(1 - own)]


def join_body(q_ref, k_ref, v_ref, got_ref, q_out, kv_out):
    side = core_side()
    for own in range(2):

        @pl.when(side == own)
        def _():
            mine = slice(own * HD, (own + 1) * HD)
            theirs = slice((1 - own) * HD, (2 - own) * HD)
            q_out[mine, :] = q_ref[:, half(own)]
            q_out[theirs, :] = got_ref[0]
            for i, ref in enumerate((k_ref, v_ref)):
                kv_out[i, mine, :] = ref[:, half(own)]
                kv_out[i, theirs, :] = got_ref[i + 1]


def att_dout_body(d0, d1, d2, d3, w_ref, keep_ref, send_ref):
    dout = project((d0, d1, d2, d3), w_ref, shard_owners(), d0.shape[1])
    side = core_side()
    for own in range(2):

        @pl.when(side == own)
        def _():
            keep_ref[...] = dout[:, half(own)]
            send_ref[...] = dout[:, half(1 - own)]


def join_dout_body(q_ref, keep_ref, got_ref, qd_out):
    side = core_side()
    qd_out[0] = q_ref[...]
    for own in range(2):

        @pl.when(side == own)
        def _():
            qd_out[1, own * HD : (own + 1) * HD, :] = keep_ref[...]
            qd_out[1, (1 - own) * HD : (2 - own) * HD, :] = got_ref[...]


def att_rows_body(qd_ref, kv0, kv1, kv2, kv3, kv4, dq_ref, stat_ref):
    chip = (lax.axis_index("seq") // 2) % (lax.axis_size("seq") // 2 // DOCS)
    rows, cols = grid_ids(PAIR, PAIR)
    near = cols <= rows
    scale = 1.0 / math.sqrt(HD)
    blocks = (kv0, kv1, kv2, kv3, kv4)
    lanes = lax.broadcasted_iota(jnp.int32, (PAIR, HD), 1)
    stats = jnp.zeros((PAIR, HD), F32)
    for h in range(2):
        hc = head_cols(h)
        q = qd_ref[0, :, hc]
        dout = qd_ref[1, :, hc]
        raw = [dot(q, kv[0, :, hc], NT) * scale for kv in blocks]
        edge = jnp.where(near, raw[0], jnp.where(chip >= RING, raw[RING], FAR))
        scores = [edge] + [jnp.where(chip >= s, raw[s], FAR) for s in range(1, RING)]
        top = scores[0]
        for part in scores[1:]:
            top = jnp.maximum(top, part)
        top = jnp.max(top, axis=1, keepdims=True)
        expo = [jnp.exp(part - top) for part in scores]
        mass = jnp.sum(expo[0] + expo[1] + expo[2] + expo[3], axis=1, keepdims=True)
        inv = 1.0 / mass
        probs = [e * inv for e in expo]
        dp = [dot(dout, kv[1, :, hc], NT) for kv in blocks]
        dprob = [jnp.where(near, dp[0], dp[RING])] + dp[1:RING]
        spread = probs[0] * dprob[0]
        for s in range(1, RING):
            spread = spread + probs[s] * dprob[s]
        row_dot = jnp.sum(spread, axis=1, keepdims=True)
        dscore = [p * (d - row_dot) for p, d in zip(probs, dprob)]
        grad = dot(jnp.where(near, dscore[0], 0.0).astype(BF16), kv0[0, :, hc], NN)
        grad = grad + dot(jnp.where(near, 0.0, dscore[0]).astype(BF16), kv4[0, :, hc], NN)
        for s in range(1, RING):
            grad = grad + dot(dscore[s].astype(BF16), blocks[s][0, :, hc], NN)
        dq_ref[:, hc] = (grad * scale).astype(BF16)
        for i, col in enumerate((top, inv, row_dot)):
            stats = jnp.where(lanes == 3 * h + i, col, stats)
    stat_ref[...] = stats.T[:8]


def att_cols_body(
    kv_ref, dq_ref, qd0, qd1, qd2, qd3, qd4, st0, st1, st2, st3, st4, keep_ref, send_ref, out_ref
):
    rows, cols = grid_ids(PAIR, PAIR)
    near = rows <= cols
    scale = 1.0 / math.sqrt(HD)
    out_ref[0] = dq_ref[...]
    for h in range(2):
        hc = head_cols(h)
        k = kv_ref[0, :, hc]
        v = kv_ref[1, :, hc]
        dk = jnp.zeros((PAIR, HD), F32)
        dv = jnp.zeros((PAIR, HD), F32)
        for s, (qd, st) in enumerate(zip((qd0, qd1, qd2, qd3, qd4), (st0, st1, st2, st3, st4))):
            q = qd[0, :, hc]
            dout = qd[1, :, hc]
            stats = st[...]
            shifted = dot(k, q, NT) * scale - stats[3 * h : 3 * h + 1]
            if s == 0:
                shifted = jnp.where(near, shifted, FAR)
            if s == RING:
                shifted = jnp.where(near, FAR, shifted)
            probs = jnp.exp(shifted) * stats[3 * h + 1 : 3 * h + 2]
            dscore = probs * (dot(v, dout, NT) - stats[3 * h + 2 : 3 * h + 3])
            dk = dk + dot(dscore.astype(BF16), q, NN)
            dv = dv + dot(probs.astype(BF16), dout, NN)
        out_ref[1, :, hc] = (dk * scale).astype(BF16)
        out_ref[2, :, hc] = dv.astype(BF16)
    side = core_side()
    for own in range(2):

        @pl.when(side == own)
        def _():
            keep_ref[...] = out_ref[:, own * HD : (own + 1) * HD, :]
            send_ref[...] = out_ref[:, (1 - own) * HD : (2 - own) * HD, :]


def finish_body(keep_ref, got_ref, dq_ref, dk_ref, dv_ref):
    side = core_side()
    for own in range(2):

        @pl.when(side == own)
        def _():
            for i, ref in enumerate((dq_ref, dk_ref, dv_ref)):
                ref[:, half(own)] = keep_ref[i]
                ref[:, half(1 - own)] = got_ref[i]


def kernel(body, outs, name, flops=0, scratch=()):
    shapes = [jax.ShapeDtypeStruct(shape, dtype) for shape, dtype in outs]
    nbytes = sum(math.prod(s.shape) * s.dtype.itemsize for s in shapes)
    return pl.pallas_call(
        body,
        out_shape=shapes if len(shapes) > 1 else shapes[0],
        scratch_shapes=list(scratch),
        compiler_params=pltpu.CompilerParams(vmem_limit_bytes=48 * 1024 * 1024),
        cost_estimate=pl.CostEstimate(flops=flops, bytes_accessed=2 * nbytes, transcendentals=0),
        name=name,
    )


def bind(body, **fixed):
    def bound(*refs):
        return body(*refs, **fixed)

    return bound


def shards(
    att_q, att_k, att_v, att_dy, att_out_w,
    gdn_q, gdn_k, gdn_v, gdn_beta, gdn_gate, gdn_state, gdn_dy, gdn_out_w,
):
    toks, width = att_q.shape
    heads = width // HD
    seq_count = lax.axis_size("seq")
    head_count = lax.axis_size("head")
    per_doc = seq_count // DOCS
    swap = [(i, i ^ 1) for i in range(seq_count)]
    forth = [(i, i + 2) for i in range(seq_count - 2) if i // per_doc == (i + 2) // per_doc]
    back = [(j, i) for i, j in forth]

    def gathered(value):
        return [value] + [
            lax.ppermute(value, "head", [(i, (i + s) % head_count) for i in range(head_count)])
            for s in range(1, head_count)
        ]

    gdn_parts = gathered(gdn_dy)
    send = kernel(pack_body, [((3, toks, PAIR), BF16)], "att_pack")(att_q, att_k, att_v)
    got = lax.ppermute(send, "seq", swap)
    att_parts = gathered(att_dy)
    q_pair, kv_pair = kernel(
        join_body, [((PAIR, PAIR), BF16), ((2, PAIR, PAIR), BF16)], "att_join"
    )(att_q, att_k, att_v, got)
    kv = [kv_pair]
    for _ in range(RING):
        kv.append(lax.ppermute(kv[-1], "seq", forth))

    inverse, n_map, delta = kernel(
        bind(gdn_pre_body, heads=heads),
        [((heads, HD, HD), F32), ((heads, HD, HD), F32), ((heads, HD + 16, HD), BF16)],
        "gdn_pre", flops=3 * 10**9,
    )(gdn_q, gdn_k, gdn_beta, gdn_gate)
    gdn_dout, payload = kernel(
        bind(gdn_dout_body, heads=heads),
        [((toks, width), BF16), ((heads, 2 * HD + 16, HD), BF16)],
        "gdn_dout", flops=10**9,
    )(*gdn_parts, gdn_out_w, n_map, delta)

    quads = [[SEG * i + j for j in range(SEG)] for i in range(seq_count // SEG)]
    blocks = lax.all_to_all(payload, "seq", 0, 0, axis_index_groups=quads)
    folded = kernel(chain_fold_body, [((2 * HD + 16, HD), BF16)], "chain_fold")(blocks)
    later = [
        lax.ppermute(
            folded, "seq",
            [(i, i - SEG * s) for i in range(seq_count) if i % per_doc >= SEG * s],
        )
        for s in range(1, SEGS)
    ]
    walked = kernel(chain_walk_body, [((SEG, HD, HD), BF16)], "chain_walk")(*later, blocks)
    adjoint = lax.all_to_all(walked, "seq", 0, 0, axis_index_groups=quads)
    gdn_dq, gdn_dk, gdn_dv, gdn_dbeta, gdn_dgate = kernel(
        bind(gdn_post_body, heads=heads),
        [((toks, width), BF16)] * 3 + [((heads, toks), F32)] * 2,
        "gdn_post", flops=5 * 10**9,
    )(gdn_q, gdn_k, gdn_v, gdn_beta, gdn_gate, gdn_state[0], inverse, gdn_dout, adjoint)

    dout_keep, dout_send = kernel(
        att_dout_body, [((toks, PAIR), BF16)] * 2, "att_dout", flops=10**9
    )(*att_parts, att_out_w)
    dout_got = lax.ppermute(dout_send, "seq", swap)
    qd = [kernel(join_dout_body, [((2, PAIR, PAIR), BF16)], "att_join_dout")(q_pair, dout_keep, dout_got)]
    for _ in range(RING):
        qd.append(lax.ppermute(qd[-1], "seq", back))
    dq_pair, stats = kernel(
        att_rows_body, [((PAIR, PAIR), BF16), ((8, PAIR), F32)], "att_rows", flops=3 * 10**9
    )(qd[0], *kv)
    all_stats = [stats] + [
        lax.ppermute(
            stats, "seq",
            [(i, i - 2 * s) for i in range(seq_count) if i % per_doc >= 2 * s],
        )
        for s in range(1, RING + 1)
    ]
    keep, send = kernel(
        att_cols_body, [((3, toks, PAIR), BF16)] * 2, "att_cols", flops=3 * 10**9,
        scratch=[pltpu.VMEM((3, PAIR, PAIR), BF16)],
    )(kv_pair, dq_pair, *qd, *all_stats)
    got = lax.ppermute(send, "seq", swap)
    att_dq, att_dk, att_dv = kernel(finish_body, [((toks, width), BF16)] * 3, "att_finish")(keep, got)
    return (att_dq, att_dk, att_dv, gdn_dq, gdn_dk, gdn_dv, gdn_dbeta, gdn_dgate)


def solution(mesh):
    tokens = P("seq", "head")
    rates = P("head", "seq")
    weight = P("head", None)
    return jax.shard_map(
        shards,
        mesh=mesh,
        in_specs=(
            tokens, tokens, tokens, tokens, weight,
            tokens, tokens, tokens, rates, rates, P("seq", "head", None, None), tokens, weight,
        ),
        out_specs=(tokens, tokens, tokens, tokens, tokens, tokens, rates, rates),
        check_vma=False,
    )
```

```python
import math

import jax
import jax.numpy as jnp
from jax import lax
from jax.experimental import pallas as pl
from jax.experimental.pallas import tpu as pltpu
from jax.sharding import PartitionSpec as P

HD = 128
PAIR = 256
RING = 4
SEG = 8
SEGS = 4
DOCS = 2
F32 = jnp.float32
BF16 = jnp.bfloat16
NN = (((1,), (0,)), ((), ()))
NT = (((1,), (1,)), ((), ()))
TN = (((0,), (0,)), ((), ()))
FAR = -1e30


def dot(left, right, dims):
    return lax.dot_general(left, right, dims, preferred_element_type=F32)


def exact(left, right, dims):
    return lax.dot_general(
        left, right, dims, precision=lax.Precision.HIGHEST, preferred_element_type=F32
    )


def split(value):
    high = value.astype(BF16)
    return high, (value - high.astype(F32)).astype(BF16)


def dot_l(left, right, dims):
    high, low = split(left)
    return dot(high, right, dims) + dot(low, right, dims)


def dot_r(left, right, dims):
    high, low = split(right)
    return dot(left, high, dims) + dot(left, low, dims)


def dot3(left, right, dims):
    lh, ll = split(left)
    rh, rl = split(right)
    return dot(lh, rh, dims) + (dot(lh, rl, dims) + dot(ll, rh, dims))


def grid_ids(rows, cols):
    return (
        lax.broadcasted_iota(jnp.int32, (rows, cols), 0),
        lax.broadcasted_iota(jnp.int32, (rows, cols), 1),
    )


def head_cols(head):
    return slice(head * HD, (head + 1) * HD)


def token_rates(beta, gate, heads):
    rows, cols = grid_ids(HD, HD)
    pad = jnp.zeros((8 - heads, HD), F32)
    beta8 = jnp.concatenate([beta, pad])
    gate8 = jnp.concatenate([gate, pad])
    upto = (rows <= cols).astype(F32)
    crow = exact(gate8, upto, NN)
    ccol = exact((cols <= rows).astype(F32), gate8, NT)
    bcol = exact((cols == rows).astype(F32), beta8, NT)
    return crow, ccol, bcol, beta8


def gdn_pre_body(q_ref, k_ref, beta_ref, gate_ref, m_ref, n_ref, delta_ref, *, heads):
    rows, cols = grid_ids(HD, HD)
    crow, ccol, bcol, brow = token_rates(beta_ref[...], gate_ref[...], heads)
    lower = rows >= cols
    strict = rows > cols
    eye = (rows == cols).astype(F32)
    systems = []
    mixes = []
    for h in range(heads):
        k = k_ref[:, head_cols(h)]
        q = q_ref[:, head_cols(h)]
        decay = jnp.exp(jnp.minimum(ccol[:, h : h + 1] - crow[h : h + 1, :], 0.0))
        systems.append(jnp.where(strict, bcol[:, h : h + 1] * decay * dot(k, k, NT), 0.0))
        mixes.append(jnp.where(lower, decay * dot(q, k, NT), 0.0))
    pair = (rows >> 1) == (cols >> 1)
    inverse = [eye - jnp.where(pair, s, 0.0) for s in systems]
    for level in range(1, 7):
        ring = ((rows >> (level + 1)) == (cols >> (level + 1))) & ((rows >> level) != (cols >> level))
        part = [dot3(m, jnp.where(ring, s, 0.0), NN) for m, s in zip(inverse, systems)]
        inverse = [m - dot3(x, m, NN) for m, x in zip(inverse, part)]
    for h in range(heads):
        k = k_ref[:, head_cols(h)]
        q = q_ref[:, head_cols(h)]
        last = crow[h : h + 1, HD - 1 :]
        grow = jnp.exp(crow[h : h + 1, :])
        gcol = jnp.exp(ccol[:, h : h + 1])
        tcol = jnp.exp(jnp.minimum(last - ccol[:, h : h + 1], 0.0))
        wy = dot_l(inverse[h] * (brow[h : h + 1, :] * grow), k, NN)
        m_ref[h] = inverse[h]
        n_ref[h] = gcol * q.astype(F32) - dot3(mixes[h], wy, NN)
        delta_ref[h, :HD, :] = dot_r(k, tcol * wy, TN).astype(BF16)
        total = jnp.broadcast_to(jnp.exp(last), (16, HD))
        high = total.astype(BF16).astype(F32)
        mid = (total - high).astype(BF16).astype(F32)
        low = total - high - mid
        tile_row = lax.broadcasted_iota(jnp.int32, (16, HD), 0)
        tile = jnp.where(
            tile_row == 0, high, jnp.where(tile_row == 1, mid, jnp.where(tile_row == 2, low, 0.0))
        )
        delta_ref[h, HD:, :] = tile.astype(BF16)


def project(parts, w_ref, owners, width):
    total = None
    for part, owner in zip(parts, owners):
        span = pl.ds(pl.multiple_of(owner * width, width), width)
        term = dot(part[...], w_ref[:, span], NT)
        total = term if total is None else total + term
    return total.astype(BF16)


def shard_owners():
    own = lax.axis_index("head")
    count = lax.axis_size("head")
    return [(own - shift + count) % count for shift in range(count)]


def gdn_dout_body(d0, d1, d2, d3, w_ref, n_ref, delta_ref, dout_ref, send_ref, *, heads):
    dout = project((d0, d1, d2, d3), w_ref, shard_owners(), d0.shape[1])
    dout_ref[...] = dout
    part = HD * heads // SEG
    for h in range(heads):
        local = dot_r(dout[:, head_cols(h)], n_ref[h], TN).astype(BF16)
        for i in range(HD // part):
            slot = h * (HD // part) + i
            send_ref[slot, : HD + 16, :] = delta_ref[h]
            send_ref[slot, HD + 16 :, :] = local[i * part : (i + 1) * part]


def unpack_map(payload):
    delta = payload[:HD]
    tile = payload[HD : HD + 16].astype(F32)
    gain = tile[0:1] + tile[1:2] + tile[2:3]
    return gain, delta, payload[HD + 16 :].astype(F32)


def chain_fold_body(blocks_ref, out_ref):
    gain, delta, local = unpack_map(blocks_ref[SEG - 1])
    both = jnp.concatenate([delta.astype(F32), local])
    for b in range(SEG - 2, -1, -1):
        next_gain, next_delta, next_local = unpack_map(blocks_ref[b])
        moved = next_gain * both - dot_l(both, next_delta, NN)
        both = moved + jnp.concatenate([gain * next_delta.astype(F32), next_local])
        gain = gain * next_gain
    out_ref[:HD, :] = both[:HD].astype(BF16)
    out_ref[HD + 16 :, :] = both[HD:].astype(BF16)
    total = jnp.broadcast_to(gain, (16, HD))
    high = total.astype(BF16).astype(F32)
    mid = (total - high).astype(BF16).astype(F32)
    low = total - high - mid
    tile_row = lax.broadcasted_iota(jnp.int32, (16, HD), 0)
    tile = jnp.where(
        tile_row == 0, high, jnp.where(tile_row == 1, mid, jnp.where(tile_row == 2, low, 0.0))
    )
    out_ref[HD : HD + 16, :] = tile.astype(BF16)


def chain_walk_body(*refs):
    later, blocks_ref, out_ref = refs[: SEGS - 1], refs[SEGS - 1], refs[SEGS]
    part = out_ref.shape[1]
    adjoint = jnp.zeros((part, HD), F32)

    def step(adjoint, payload):
        gain, delta, local = unpack_map(payload)
        high, low = split(adjoint)
        both = dot(jnp.concatenate([high, low]), delta, NN)
        return gain * adjoint - (both[:part] + both[part:]) + local

    for seg in range(SEGS - 2, -1, -1):
        adjoint = step(adjoint, later[seg][...])
    for b in range(SEG - 1, -1, -1):
        out_ref[b] = adjoint.astype(BF16)
        if b:
            adjoint = step(adjoint, blocks_ref[b])


def gdn_post_body(
    q_ref, k_ref, v_ref, beta_ref, gate_ref, s_ref, m_ref, dout_ref, a_ref,
    dq_ref, dk_ref, dv_ref, dbeta_ref, dgate_ref, *, heads,
):
    rows, cols = grid_ids(HD, HD)
    crow, ccol, bcol, _ = token_rates(beta_ref[...], gate_ref[...], heads)
    lower = rows >= cols
    strict = rows > cols
    after = jnp.zeros((HD, HD), F32)
    before = jnp.zeros((HD, HD), F32)
    rates = jnp.zeros((HD, HD), F32)
    row8 = lax.broadcasted_iota(jnp.int32, (8, HD), 0)
    taken = jnp.zeros((8, HD), F32)
    whole = jnp.zeros((8, HD), F32)
    for h in range(heads):
        q = q_ref[:, head_cols(h)]
        k = k_ref[:, head_cols(h)]
        v = v_ref[:, head_cols(h)].astype(F32)
        dout = dout_ref[:, head_cols(h)]
        state = s_ref[h]
        inverse = m_ref[h]
        adjoint = a_ref[h]
        b = bcol[:, h : h + 1]
        c = ccol[:, h : h + 1]
        last = crow[h : h + 1, HD - 1 :]
        g = jnp.exp(c)
        t = jnp.exp(jnp.minimum(last - c, 0.0))
        decay = jnp.where(lower, jnp.exp(jnp.minimum(c - crow[h : h + 1, :], 0.0)), 0.0)
        gram = decay * dot(k, k, NT)
        mix = decay * dot(q, k, NT)
        k_s = dot_r(k, state, NT)
        q_s = dot_r(q, state, NT)
        resid = v - g * k_s
        fresh = dot3(inverse, b * resid, NN)
        k_a = dot(k, adjoint, NT)
        dfresh = dot_l(mix, dout, TN) + t * k_a
        dright = dot3(inverse, dfresh, TN)
        dmix = dot_r(dout, fresh, NT)
        dsys = jnp.where(strict, -dot3(dright, fresh, NT), 0.0)
        x_mix = dmix * decay
        x_sys = dsys * (b * decay)
        dq_ref[:, head_cols(h)] = (g * dot_r(dout, state, NN) + dot_l(x_mix, k, NN)).astype(BF16)
        dk = dot_l(x_mix, q, TN) + dot_l(x_sys, k, NN) + dot_l(x_sys, k, TN)
        dk = dk + dot_l(t * fresh, adjoint, NN) - dot3((b * g) * dright, state, NN)
        dk_ref[:, head_cols(h)] = dk.astype(BF16)
        dv_ref[:, head_cols(h)] = (b * dright).astype(BF16)
        dbeta = jnp.sum(dright * resid + dsys * gram, axis=1, keepdims=True)
        flow = dmix * mix + dsys * (b * gram)
        dgrow = jnp.sum(
            g * (dout.astype(F32) * q_s - b * dright * k_s) + flow, axis=1, keepdims=True
        )
        dtail = jnp.sum(t * fresh * k_a, axis=1, keepdims=True)
        ends = jnp.exp(last) * jnp.sum(
            jnp.sum(adjoint.astype(F32) * state, axis=1, keepdims=True), axis=0, keepdims=True
        )
        after = jnp.where(cols == h, dgrow, after)
        before = jnp.where(cols == h, dtail, before)
        rates = jnp.where(cols == h, dbeta, rates)
        taken = jnp.where(row8 == h, jnp.sum(flow, axis=0, keepdims=True), taken)
        whole = jnp.where(row8 == h, ends, whole)
    not_before = (rows >= cols).astype(F32)
    dgate = exact(after, not_before, TN) + exact(before, (rows < cols).astype(F32), TN)
    dgate = dgate[:8] + whole - exact(taken, not_before, NN)
    dgate_ref[...] = dgate[:heads]
    dbeta_ref[...] = exact(rates, (rows == cols).astype(F32), TN)[:heads]


def core_side():
    return lax.axis_index("seq") % 2


def half(side):
    return slice(side * PAIR, (side + 1) * PAIR)


def pack_body(q_ref, k_ref, v_ref, send_ref):
    side = core_side()
    for own in range(2):

        @pl.when(side == own)
        def _():
            for i, ref in enumerate((q_ref, k_ref, v_ref)):
                send_ref[i] = ref[:, half(1 - own)]


def join_body(q_ref, k_ref, v_ref, got_ref, q_out, kv_out):
    side = core_side()
    for own in range(2):

        @pl.when(side == own)
        def _():
            mine = slice(own * HD, (own + 1) * HD)
            theirs = slice((1 - own) * HD, (2 - own) * HD)
            q_out[mine, :] = q_ref[:, half(own)]
            q_out[theirs, :] = got_ref[0]
            for i, ref in enumerate((k_ref, v_ref)):
                kv_out[i, mine, :] = ref[:, half(own)]
                kv_out[i, theirs, :] = got_ref[i + 1]


def att_dout_body(d0, d1, d2, d3, w_ref, keep_ref, send_ref):
    dout = project((d0, d1, d2, d3), w_ref, shard_owners(), d0.shape[1])
    side = core_side()
    for own in range(2):

        @pl.when(side == own)
        def _():
            keep_ref[...] = dout[:, half(own)]
            send_ref[...] = dout[:, half(1 - own)]


def join_dout_body(q_ref, keep_ref, got_ref, qd_out):
    side = core_side()
    qd_out[0] = q_ref[...]
    for own in range(2):

        @pl.when(side == own)
        def _():
            qd_out[1, own * HD : (own + 1) * HD, :] = keep_ref[...]
            qd_out[1, (1 - own) * HD : (2 - own) * HD, :] = got_ref[...]


def att_rows_body(qd_ref, kv0, kv1, kv2, kv3, kv4, dq_ref, stat_ref):
    chip = (lax.axis_index("seq") // 2) % (lax.axis_size("seq") // 2 // DOCS)
    rows, cols = grid_ids(PAIR, PAIR)
    near = cols <= rows
    scale = 1.0 / math.sqrt(HD)
    blocks = (kv0, kv1, kv2, kv3, kv4)
    lanes = lax.broadcasted_iota(jnp.int32, (PAIR, HD), 1)
    stats = jnp.zeros((PAIR, HD), F32)
    for h in range(2):
        hc = head_cols(h)
        q = qd_ref[0, :, hc]
        dout = qd_ref[1, :, hc]
        raw = [dot(q, kv[0, :, hc], NT) * scale for kv in blocks]
        edge = jnp.where(near, raw[0], jnp.where(chip >= RING, raw[RING], FAR))
        scores = [edge] + [jnp.where(chip >= s, raw[s], FAR) for s in range(1, RING)]
        top = scores[0]
        for part in scores[1:]:
            top = jnp.maximum(top, part)
        top = jnp.max(top, axis=1, keepdims=True)
        expo = [jnp.exp(part - top) for part in scores]
        mass = jnp.sum(expo[0] + expo[1] + expo[2] + expo[3], axis=1, keepdims=True)
        inv = 1.0 / mass
        probs = [e * inv for e in expo]
        dp = [dot(dout, kv[1, :, hc], NT) for kv in blocks]
        dprob = [jnp.where(near, dp[0], dp[RING])] + dp[1:RING]
        spread = probs[0] * dprob[0]
        for s in range(1, RING):
            spread = spread + probs[s] * dprob[s]
        row_dot = jnp.sum(spread, axis=1, keepdims=True)
        dscore = [p * (d - row_dot) for p, d in zip(probs, dprob)]
        grad = dot(jnp.where(near, dscore[0], 0.0).astype(BF16), kv0[0, :, hc], NN)
        grad = grad + dot(jnp.where(near, 0.0, dscore[0]).astype(BF16), kv4[0, :, hc], NN)
        for s in range(1, RING):
            grad = grad + dot(dscore[s].astype(BF16), blocks[s][0, :, hc], NN)
        dq_ref[:, hc] = (grad * scale).astype(BF16)
        for i, col in enumerate((top, inv, row_dot)):
            stats = jnp.where(lanes == 3 * h + i, col, stats)
    stat_ref[...] = stats.T[:8]


def att_cols_body(
    kv_ref, dq_ref, qd0, qd1, qd2, qd3, qd4, st0, st1, st2, st3, st4, keep_ref, send_ref, out_ref
):
    rows, cols = grid_ids(PAIR, PAIR)
    near = rows <= cols
    scale = 1.0 / math.sqrt(HD)
    out_ref[0] = dq_ref[...]
    for h in range(2):
        hc = head_cols(h)
        k = kv_ref[0, :, hc]
        v = kv_ref[1, :, hc]
        dk = jnp.zeros((PAIR, HD), F32)
        dv = jnp.zeros((PAIR, HD), F32)
        for s, (qd, st) in enumerate(zip((qd0, qd1, qd2, qd3, qd4), (st0, st1, st2, st3, st4))):
            q = qd[0, :, hc]
            dout = qd[1, :, hc]
            stats = st[...]
            shifted = dot(k, q, NT) * scale - stats[3 * h : 3 * h + 1]
            if s == 0:
                shifted = jnp.where(near, shifted, FAR)
            if s == RING:
                shifted = jnp.where(near, FAR, shifted)
            probs = jnp.exp(shifted) * stats[3 * h + 1 : 3 * h + 2]
            dscore = probs * (dot(v, dout, NT) - stats[3 * h + 2 : 3 * h + 3])
            dk = dk + dot(dscore.astype(BF16), q, NN)
            dv = dv + dot(probs.astype(BF16), dout, NN)
        out_ref[1, :, hc] = (dk * scale).astype(BF16)
        out_ref[2, :, hc] = dv.astype(BF16)
    side = core_side()
    for own in range(2):

        @pl.when(side == own)
        def _():
            keep_ref[...] = out_ref[:, own * HD : (own + 1) * HD, :]
            send_ref[...] = out_ref[:, (1 - own) * HD : (2 - own) * HD, :]


def finish_body(keep_ref, got_ref, dq_ref, dk_ref, dv_ref):
    side = core_side()
    for own in range(2):

        @pl.when(side == own)
        def _():
            for i, ref in enumerate((dq_ref, dk_ref, dv_ref)):
                ref[:, half(own)] = keep_ref[i]
                ref[:, half(1 - own)] = got_ref[i]


def kernel(body, outs, name, flops=0, scratch=()):
    shapes = [jax.ShapeDtypeStruct(shape, dtype) for shape, dtype in outs]
    nbytes = sum(math.prod(s.shape) * s.dtype.itemsize for s in shapes)
    return pl.pallas_call(
        body,
        out_shape=shapes if len(shapes) > 1 else shapes[0],
        scratch_shapes=list(scratch),
        compiler_params=pltpu.CompilerParams(vmem_limit_bytes=48 * 1024 * 1024),
        cost_estimate=pl.CostEstimate(flops=flops, bytes_accessed=2 * nbytes, transcendentals=0),
        name=name,
    )


def bind(body, **fixed):
    def bound(*refs):
        return body(*refs, **fixed)

    return bound


def shards(
    att_q, att_k, att_v, att_dy, att_out_w,
    gdn_q, gdn_k, gdn_v, gdn_beta, gdn_gate, gdn_state, gdn_dy, gdn_out_w,
):
    toks, width = att_q.shape
    heads = width // HD
    seq_count = lax.axis_size("seq")
    head_count = lax.axis_size("head")
    per_doc = seq_count // DOCS
    swap = [(i, i ^ 1) for i in range(seq_count)]
    forth = [(i, i + 2) for i in range(seq_count - 2) if i // per_doc == (i + 2) // per_doc]
    back = [(j, i) for i, j in forth]

    def gathered(value):
        return [value] + [
            lax.ppermute(value, "head", [(i, (i + s) % head_count) for i in range(head_count)])
            for s in range(1, head_count)
        ]

    gdn_parts = gathered(gdn_dy)
    send = kernel(pack_body, [((3, toks, PAIR), BF16)], "att_pack")(att_q, att_k, att_v)
    got = lax.ppermute(send, "seq", swap)
    att_parts = gathered(att_dy)
    q_pair, kv_pair = kernel(
        join_body, [((PAIR, PAIR), BF16), ((2, PAIR, PAIR), BF16)], "att_join"
    )(att_q, att_k, att_v, got)
    kv = [kv_pair]
    for _ in range(RING):
        kv.append(lax.ppermute(kv[-1], "seq", forth))

    inverse, n_map, delta = kernel(
        bind(gdn_pre_body, heads=heads),
        [((heads, HD, HD), F32), ((heads, HD, HD), F32), ((heads, HD + 16, HD), BF16)],
        "gdn_pre", flops=3 * 10**9,
    )(gdn_q, gdn_k, gdn_beta, gdn_gate)
    gdn_dout, payload = kernel(
        bind(gdn_dout_body, heads=heads),
        [((toks, width), BF16), ((SEG, HD + 16 + HD * heads // SEG, HD), BF16)],
        "gdn_dout", flops=10**9,
    )(*gdn_parts, gdn_out_w, n_map, delta)

    quads = [[SEG * i + j for j in range(SEG)] for i in range(seq_count // SEG)]
    blocks = lax.all_to_all(payload, "seq", 0, 0, axis_index_groups=quads)
    folded = kernel(chain_fold_body, [(blocks.shape[1:], BF16)], "chain_fold")(blocks)
    later = [
        lax.ppermute(
            folded, "seq",
            [(i, i - SEG * s) for i in range(seq_count) if i % per_doc >= SEG * s],
        )
        for s in range(1, SEGS)
    ]
    walked = kernel(chain_walk_body, [((SEG, HD * heads // SEG, HD), BF16)], "chain_walk")(*later, blocks)
    adjoint = lax.all_to_all(walked, "seq", 0, 0, axis_index_groups=quads).reshape(heads, HD, HD)
    gdn_dq, gdn_dk, gdn_dv, gdn_dbeta, gdn_dgate = kernel(
        bind(gdn_post_body, heads=heads),
        [((toks, width), BF16)] * 3 + [((heads, toks), F32)] * 2,
        "gdn_post", flops=5 * 10**9,
    )(gdn_q, gdn_k, gdn_v, gdn_beta, gdn_gate, gdn_state[0], inverse, gdn_dout, adjoint)

    dout_keep, dout_send = kernel(
        att_dout_body, [((toks, PAIR), BF16)] * 2, "att_dout", flops=10**9
    )(*att_parts, att_out_w)
    dout_got = lax.ppermute(dout_send, "seq", swap)
    qd = [kernel(join_dout_body, [((2, PAIR, PAIR), BF16)], "att_join_dout")(q_pair, dout_keep, dout_got)]
    for _ in range(RING):
        qd.append(lax.ppermute(qd[-1], "seq", back))
    dq_pair, stats = kernel(
        att_rows_body, [((PAIR, PAIR), BF16), ((8, PAIR), F32)], "att_rows", flops=3 * 10**9
    )(qd[0], *kv)
    all_stats = [stats] + [
        lax.ppermute(
            stats, "seq",
            [(i, i - 2 * s) for i in range(seq_count) if i % per_doc >= 2 * s],
        )
        for s in range(1, RING + 1)
    ]
    keep, send = kernel(
        att_cols_body, [((3, toks, PAIR), BF16)] * 2, "att_cols", flops=3 * 10**9,
        scratch=[pltpu.VMEM((3, PAIR, PAIR), BF16)],
    )(kv_pair, dq_pair, *qd, *all_stats)
    got = lax.ppermute(send, "seq", swap)
    att_dq, att_dk, att_dv = kernel(finish_body, [((toks, width), BF16)] * 3, "att_finish")(keep, got)
    return (att_dq, att_dk, att_dv, gdn_dq, gdn_dk, gdn_dv, gdn_dbeta, gdn_dgate)


def solution(mesh):
    tokens = P("seq", "head")
    rates = P("head", "seq")
    weight = P("head", None)
    return jax.shard_map(
        shards,
        mesh=mesh,
        in_specs=(
            tokens, tokens, tokens, tokens, weight,
            tokens, tokens, tokens, rates, rates, P("seq", "head", None, None), tokens, weight,
        ),
        out_specs=(tokens, tokens, tokens, tokens, tokens, tokens, rates, rates),
        check_vma=False,
    )
```

```python
import math

import jax
import jax.numpy as jnp
from jax import lax
from jax.experimental import pallas as pl
from jax.experimental.pallas import tpu as pltpu
from jax.sharding import PartitionSpec as P

HD = 128
PAIR = 256
RING = 4
SEG = 8
SEGS = 4
DOCS = 2
F32 = jnp.float32
BF16 = jnp.bfloat16
NN = (((1,), (0,)), ((), ()))
NT = (((1,), (1,)), ((), ()))
TN = (((0,), (0,)), ((), ()))
FAR = -1e30


def dot(left, right, dims):
    return lax.dot_general(left, right, dims, preferred_element_type=F32)


def exact(left, right, dims):
    return lax.dot_general(
        left, right, dims, precision=lax.Precision.HIGHEST, preferred_element_type=F32
    )


def split(value):
    high = value.astype(BF16)
    return high, (value - high.astype(F32)).astype(BF16)


def dot_l(left, right, dims):
    high, low = split(left)
    return dot(high, right, dims) + dot(low, right, dims)


def dot_r(left, right, dims):
    high, low = split(right)
    return dot(left, high, dims) + dot(left, low, dims)


def dot3(left, right, dims):
    lh, ll = split(left)
    rh, rl = split(right)
    return dot(lh, rh, dims) + (dot(lh, rl, dims) + dot(ll, rh, dims))


def grid_ids(rows, cols):
    return (
        lax.broadcasted_iota(jnp.int32, (rows, cols), 0),
        lax.broadcasted_iota(jnp.int32, (rows, cols), 1),
    )


def head_cols(head):
    return slice(head * HD, (head + 1) * HD)


def token_rates(beta, gate, heads):
    rows, cols = grid_ids(HD, HD)
    pad = jnp.zeros((8 - heads, HD), F32)
    beta8 = jnp.concatenate([beta, pad])
    gate8 = jnp.concatenate([gate, pad])
    upto = (rows <= cols).astype(F32)
    crow = exact(gate8, upto, NN)
    ccol = exact((cols <= rows).astype(F32), gate8, NT)
    bcol = exact((cols == rows).astype(F32), beta8, NT)
    return crow, ccol, bcol, beta8


def gdn_pre_body(q_ref, k_ref, beta_ref, gate_ref, m_ref, n_ref, delta_ref, *, heads):
    rows, cols = grid_ids(HD, HD)
    crow, ccol, bcol, brow = token_rates(beta_ref[...], gate_ref[...], heads)
    lower = rows >= cols
    strict = rows > cols
    eye = (rows == cols).astype(F32)
    systems = []
    mixes = []
    for h in range(heads):
        k = k_ref[:, head_cols(h)]
        q = q_ref[:, head_cols(h)]
        decay = jnp.exp(jnp.minimum(ccol[:, h : h + 1] - crow[h : h + 1, :], 0.0))
        systems.append(jnp.where(strict, bcol[:, h : h + 1] * decay * dot(k, k, NT), 0.0))
        mixes.append(jnp.where(lower, decay * dot(q, k, NT), 0.0))
    pair = (rows >> 1) == (cols >> 1)
    inverse = [eye - jnp.where(pair, s, 0.0) for s in systems]
    for level in range(1, 7):
        ring = ((rows >> (level + 1)) == (cols >> (level + 1))) & ((rows >> level) != (cols >> level))
        part = [dot3(m, jnp.where(ring, s, 0.0), NN) for m, s in zip(inverse, systems)]
        inverse = [m - dot3(x, m, NN) for m, x in zip(inverse, part)]
    for h in range(heads):
        k = k_ref[:, head_cols(h)]
        q = q_ref[:, head_cols(h)]
        last = crow[h : h + 1, HD - 1 :]
        grow = jnp.exp(crow[h : h + 1, :])
        gcol = jnp.exp(ccol[:, h : h + 1])
        tcol = jnp.exp(jnp.minimum(last - ccol[:, h : h + 1], 0.0))
        wy = dot_l(inverse[h] * (brow[h : h + 1, :] * grow), k, NN)
        m_ref[h] = inverse[h]
        n_ref[h] = gcol * q.astype(F32) - dot3(mixes[h], wy, NN)
        delta_ref[h, :HD, :] = dot_r(k, tcol * wy, TN).astype(BF16)
        total = jnp.broadcast_to(jnp.exp(last), (16, HD))
        high = total.astype(BF16).astype(F32)
        mid = (total - high).astype(BF16).astype(F32)
        low = total - high - mid
        tile_row = lax.broadcasted_iota(jnp.int32, (16, HD), 0)
        tile = jnp.where(
            tile_row == 0, high, jnp.where(tile_row == 1, mid, jnp.where(tile_row == 2, low, 0.0))
        )
        delta_ref[h, HD:, :] = tile.astype(BF16)


def project(parts, w_ref, owners, width):
    total = None
    for part, owner in zip(parts, owners):
        span = pl.ds(pl.multiple_of(owner * width, width), width)
        term = dot(part[...], w_ref[:, span], NT)
        total = term if total is None else total + term
    return total.astype(BF16)


def shard_owners():
    own = lax.axis_index("head")
    count = lax.axis_size("head")
    return [(own - shift + count) % count for shift in range(count)]


def gdn_dout_body(d0, d1, d2, d3, w_ref, n_ref, delta_ref, dout_ref, send_ref, *, heads):
    dout = project((d0, d1, d2, d3), w_ref, shard_owners(), d0.shape[1])
    dout_ref[...] = dout
    part = HD * heads // SEG
    for h in range(heads):
        local = dot_r(dout[:, head_cols(h)], n_ref[h], TN).astype(BF16)
        for i in range(HD // part):
            slot = h * (HD // part) + i
            send_ref[slot, : HD + 16, :] = delta_ref[h]
            send_ref[slot, HD + 16 :, :] = local[i * part : (i + 1) * part]


def unpack_map(payload):
    delta = payload[:HD]
    tile = payload[HD : HD + 16].astype(F32)
    gain = tile[0:1] + tile[1:2] + tile[2:3]
    return gain, delta, payload[HD + 16 :].astype(F32)


def chain_fold_body(blocks_ref, out_ref):
    gain, delta, local = unpack_map(blocks_ref[SEG - 1])
    both = jnp.concatenate([delta.astype(F32), local])
    for b in range(SEG - 2, -1, -1):
        next_gain, next_delta, next_local = unpack_map(blocks_ref[b])
        moved = next_gain * both - dot_l(both, next_delta, NN)
        both = moved + jnp.concatenate([gain * next_delta.astype(F32), next_local])
        gain = gain * next_gain
    out_ref[:HD, :] = both[:HD].astype(BF16)
    out_ref[HD + 16 :, :] = both[HD:].astype(BF16)
    total = jnp.broadcast_to(gain, (16, HD))
    high = total.astype(BF16).astype(F32)
    mid = (total - high).astype(BF16).astype(F32)
    low = total - high - mid
    tile_row = lax.broadcasted_iota(jnp.int32, (16, HD), 0)
    tile = jnp.where(
        tile_row == 0, high, jnp.where(tile_row == 1, mid, jnp.where(tile_row == 2, low, 0.0))
    )
    out_ref[HD : HD + 16, :] = tile.astype(BF16)


def chain_walk_body(*refs):
    later, blocks_ref, out_ref = refs[: SEGS - 1], refs[SEGS - 1], refs[SEGS]
    part = out_ref.shape[1]
    adjoint = jnp.zeros((part, HD), F32)

    def step(adjoint, payload):
        gain, delta, local = unpack_map(payload)
        high, low = split(adjoint)
        both = dot(jnp.concatenate([high, low]), delta, NN)
        return gain * adjoint - (both[:part] + both[part:]) + local

    for seg in range(SEGS - 2, -1, -1):
        adjoint = step(adjoint, later[seg][...])
    for b in range(SEG - 1, -1, -1):
        out_ref[b] = adjoint.astype(BF16)
        if b:
            adjoint = step(adjoint, blocks_ref[b])


def gdn_post_body(
    q_ref, k_ref, v_ref, beta_ref, gate_ref, s_ref, m_ref, dout_ref, a_ref,
    dq_ref, dk_ref, dv_ref, dbeta_ref, dgate_ref, *, heads,
):
    rows, cols = grid_ids(HD, HD)
    crow, ccol, bcol, _ = token_rates(beta_ref[...], gate_ref[...], heads)
    lower = rows >= cols
    strict = rows > cols
    after = jnp.zeros((HD, HD), F32)
    before = jnp.zeros((HD, HD), F32)
    rates = jnp.zeros((HD, HD), F32)
    row8 = lax.broadcasted_iota(jnp.int32, (8, HD), 0)
    taken = jnp.zeros((8, HD), F32)
    whole = jnp.zeros((8, HD), F32)
    for h in range(heads):
        q = q_ref[:, head_cols(h)]
        k = k_ref[:, head_cols(h)]
        v = v_ref[:, head_cols(h)].astype(F32)
        dout = dout_ref[:, head_cols(h)]
        state = s_ref[h]
        inverse = m_ref[h]
        adjoint = a_ref[h]
        b = bcol[:, h : h + 1]
        c = ccol[:, h : h + 1]
        last = crow[h : h + 1, HD - 1 :]
        g = jnp.exp(c)
        t = jnp.exp(jnp.minimum(last - c, 0.0))
        decay = jnp.where(lower, jnp.exp(jnp.minimum(c - crow[h : h + 1, :], 0.0)), 0.0)
        gram = decay * dot(k, k, NT)
        mix = decay * dot(q, k, NT)
        k_s = dot_r(k, state, NT)
        q_s = dot_r(q, state, NT)
        resid = v - g * k_s
        fresh = dot3(inverse, b * resid, NN)
        k_a = dot(k, adjoint, NT)
        dfresh = dot_l(mix, dout, TN) + t * k_a
        dright = dot3(inverse, dfresh, TN)
        dmix = dot_r(dout, fresh, NT)
        dsys = jnp.where(strict, -dot3(dright, fresh, NT), 0.0)
        x_mix = dmix * decay
        x_sys = dsys * (b * decay)
        dq_ref[:, head_cols(h)] = (g * dot_r(dout, state, NN) + dot_l(x_mix, k, NN)).astype(BF16)
        dk = dot_l(x_mix, q, TN) + dot_l(x_sys, k, NN) + dot_l(x_sys, k, TN)
        dk = dk + dot_l(t * fresh, adjoint, NN) - dot3((b * g) * dright, state, NN)
        dk_ref[:, head_cols(h)] = dk.astype(BF16)
        dv_ref[:, head_cols(h)] = (b * dright).astype(BF16)
        dbeta = jnp.sum(dright * resid + dsys * gram, axis=1, keepdims=True)
        flow = dmix * mix + dsys * (b * gram)
        dgrow = jnp.sum(
            g * (dout.astype(F32) * q_s - b * dright * k_s) + flow, axis=1, keepdims=True
        )
        dtail = jnp.sum(t * fresh * k_a, axis=1, keepdims=True)
        ends = jnp.exp(last) * jnp.sum(
            jnp.sum(adjoint.astype(F32) * state, axis=1, keepdims=True), axis=0, keepdims=True
        )
        after = jnp.where(cols == h, dgrow, after)
        before = jnp.where(cols == h, dtail, before)
        rates = jnp.where(cols == h, dbeta, rates)
        taken = jnp.where(row8 == h, jnp.sum(flow, axis=0, keepdims=True), taken)
        whole = jnp.where(row8 == h, ends, whole)
    not_before = (rows >= cols).astype(F32)
    dgate = exact(after, not_before, TN) + exact(before, (rows < cols).astype(F32), TN)
    dgate = dgate[:8] + whole - exact(taken, not_before, NN)
    dgate_ref[...] = dgate[:heads]
    dbeta_ref[...] = exact(rates, (rows == cols).astype(F32), TN)[:heads]


def core_side():
    return lax.axis_index("seq") % 2


def half(side):
    return slice(side * PAIR, (side + 1) * PAIR)


def pack_body(q_ref, k_ref, v_ref, send_ref):
    side = core_side()
    for own in range(2):

        @pl.when(side == own)
        def _():
            for i, ref in enumerate((q_ref, k_ref, v_ref)):
                send_ref[i] = ref[:, half(1 - own)]


def join_body(q_ref, k_ref, v_ref, got_ref, q_out, kv_out):
    side = core_side()
    for own in range(2):

        @pl.when(side == own)
        def _():
            mine = slice(own * HD, (own + 1) * HD)
            theirs = slice((1 - own) * HD, (2 - own) * HD)
            q_out[mine, :] = q_ref[:, half(own)]
            q_out[theirs, :] = got_ref[0]
            for i, ref in enumerate((k_ref, v_ref)):
                kv_out[i, mine, :] = ref[:, half(own)]
                kv_out[i, theirs, :] = got_ref[i + 1]


def att_dout_body(d0, d1, d2, d3, w_ref, keep_ref, send_ref):
    dout = project((d0, d1, d2, d3), w_ref, shard_owners(), d0.shape[1])
    side = core_side()
    for own in range(2):

        @pl.when(side == own)
        def _():
            keep_ref[...] = dout[:, half(own)]
            send_ref[...] = dout[:, half(1 - own)]


def join_dout_body(q_ref, keep_ref, got_ref, qd_out):
    side = core_side()
    qd_out[0] = q_ref[...]
    for own in range(2):

        @pl.when(side == own)
        def _():
            qd_out[1, own * HD : (own + 1) * HD, :] = keep_ref[...]
            qd_out[1, (1 - own) * HD : (2 - own) * HD, :] = got_ref[...]


def att_rows_body(qd_ref, kv0, kv1, kv2, kv3, kv4, dq_ref, stat_ref):
    chip = (lax.axis_index("seq") // 2) % (lax.axis_size("seq") // 2 // DOCS)
    rows, cols = grid_ids(PAIR, PAIR)
    near = cols <= rows
    scale = 1.0 / math.sqrt(HD)
    blocks = (kv0, kv1, kv2, kv3, kv4)
    lanes = lax.broadcasted_iota(jnp.int32, (PAIR, HD), 1)
    stats = jnp.zeros((PAIR, HD), F32)
    for h in range(2):
        hc = head_cols(h)
        q = qd_ref[0, :, hc]
        dout = qd_ref[1, :, hc]
        raw = [dot(q, kv[0, :, hc], NT) * scale for kv in blocks]
        edge = jnp.where(near, raw[0], jnp.where(chip >= RING, raw[RING], FAR))
        scores = [edge] + [jnp.where(chip >= s, raw[s], FAR) for s in range(1, RING)]
        top = scores[0]
        for part in scores[1:]:
            top = jnp.maximum(top, part)
        top = jnp.max(top, axis=1, keepdims=True)
        expo = [jnp.exp(part - top) for part in scores]
        mass = jnp.sum(expo[0] + expo[1] + expo[2] + expo[3], axis=1, keepdims=True)
        inv = 1.0 / mass
        probs = [e * inv for e in expo]
        dp = [dot(dout, kv[1, :, hc], NT) for kv in blocks]
        dprob = [jnp.where(near, dp[0], dp[RING])] + dp[1:RING]
        spread = probs[0] * dprob[0]
        for s in range(1, RING):
            spread = spread + probs[s] * dprob[s]
        row_dot = jnp.sum(spread, axis=1, keepdims=True)
        dscore = [p * (d - row_dot) for p, d in zip(probs, dprob)]
        grad = dot(jnp.where(near, dscore[0], 0.0).astype(BF16), kv0[0, :, hc], NN)
        grad = grad + dot(jnp.where(near, 0.0, dscore[0]).astype(BF16), kv4[0, :, hc], NN)
        for s in range(1, RING):
            grad = grad + dot(dscore[s].astype(BF16), blocks[s][0, :, hc], NN)
        dq_ref[:, hc] = (grad * scale).astype(BF16)
        for i, col in enumerate((top, inv, row_dot)):
            stats = jnp.where(lanes == 3 * h + i, col, stats)
    stat_ref[...] = stats.T[:8]


def att_cols_body(
    kv_ref, dq_ref, qd0, qd1, qd2, qd3, qd4, st0, st1, st2, st3, st4, keep_ref, send_ref, out_ref
):
    rows, cols = grid_ids(PAIR, PAIR)
    near = rows <= cols
    scale = 1.0 / math.sqrt(HD)
    out_ref[0] = dq_ref[...]
    for h in range(2):
        hc = head_cols(h)
        k = kv_ref[0, :, hc]
        v = kv_ref[1, :, hc]
        dk = jnp.zeros((PAIR, HD), F32)
        dv = jnp.zeros((PAIR, HD), F32)
        for s, (qd, st) in enumerate(zip((qd0, qd1, qd2, qd3, qd4), (st0, st1, st2, st3, st4))):
            q = qd[0, :, hc]
            dout = qd[1, :, hc]
            stats = st[...]
            shifted = dot(k, q, NT) * scale - stats[3 * h : 3 * h + 1]
            if s == 0:
                shifted = jnp.where(near, shifted, FAR)
            if s == RING:
                shifted = jnp.where(near, FAR, shifted)
            probs = jnp.exp(shifted) * stats[3 * h + 1 : 3 * h + 2]
            dscore = probs * (dot(v, dout, NT) - stats[3 * h + 2 : 3 * h + 3])
            dk = dk + dot(dscore.astype(BF16), q, NN)
            dv = dv + dot(probs.astype(BF16), dout, NN)
        out_ref[1, :, hc] = (dk * scale).astype(BF16)
        out_ref[2, :, hc] = dv.astype(BF16)
    side = core_side()
    for own in range(2):

        @pl.when(side == own)
        def _():
            keep_ref[...] = out_ref[:, own * HD : (own + 1) * HD, :]
            send_ref[...] = out_ref[:, (1 - own) * HD : (2 - own) * HD, :]


def finish_body(keep_ref, got_ref, dq_ref, dk_ref, dv_ref):
    side = core_side()
    for own in range(2):

        @pl.when(side == own)
        def _():
            for i, ref in enumerate((dq_ref, dk_ref, dv_ref)):
                ref[:, half(own)] = keep_ref[i]
                ref[:, half(1 - own)] = got_ref[i]


def kernel(body, outs, name, flops=0, scratch=()):
    shapes = [jax.ShapeDtypeStruct(shape, dtype) for shape, dtype in outs]
    nbytes = sum(math.prod(s.shape) * s.dtype.itemsize for s in shapes)
    return pl.pallas_call(
        body,
        out_shape=shapes if len(shapes) > 1 else shapes[0],
        scratch_shapes=list(scratch),
        compiler_params=pltpu.CompilerParams(vmem_limit_bytes=24 * 1024 * 1024),
        cost_estimate=pl.CostEstimate(flops=flops, bytes_accessed=2 * nbytes, transcendentals=0),
        name=name,
    )


def bind(body, **fixed):
    def bound(*refs):
        return body(*refs, **fixed)

    return bound


def shards(
    att_q, att_k, att_v, att_dy, att_out_w,
    gdn_q, gdn_k, gdn_v, gdn_beta, gdn_gate, gdn_state, gdn_dy, gdn_out_w,
):
    toks, width = att_q.shape
    heads = width // HD
    seq_count = lax.axis_size("seq")
    head_count = lax.axis_size("head")
    per_doc = seq_count // DOCS
    swap = [(i, i ^ 1) for i in range(seq_count)]
    forth = [(i, i + 2) for i in range(seq_count - 2) if i // per_doc == (i + 2) // per_doc]
    back = [(j, i) for i, j in forth]

    def gathered(value):
        return [value] + [
            lax.ppermute(value, "head", [(i, (i + s) % head_count) for i in range(head_count)])
            for s in range(1, head_count)
        ]

    gdn_parts = gathered(gdn_dy)
    send = kernel(pack_body, [((3, toks, PAIR), BF16)], "att_pack")(att_q, att_k, att_v)
    got = lax.ppermute(send, "seq", swap)
    att_parts = gathered(att_dy)
    q_pair, kv_pair = kernel(
        join_body, [((PAIR, PAIR), BF16), ((2, PAIR, PAIR), BF16)], "att_join"
    )(att_q, att_k, att_v, got)
    kv = [kv_pair]
    for _ in range(RING):
        kv.append(lax.ppermute(kv[-1], "seq", forth))

    inverse, n_map, delta = kernel(
        bind(gdn_pre_body, heads=heads),
        [((heads, HD, HD), F32), ((heads, HD, HD), F32), ((heads, HD + 16, HD), BF16)],
        "gdn_pre", flops=3 * 10**9,
    )(gdn_q, gdn_k, gdn_beta, gdn_gate)
    gdn_dout, payload = kernel(
        bind(gdn_dout_body, heads=heads),
        [((toks, width), BF16), ((SEG, HD + 16 + HD * heads // SEG, HD), BF16)],
        "gdn_dout", flops=10**9,
    )(*gdn_parts, gdn_out_w, n_map, delta)

    quads = [[SEG * i + j for j in range(SEG)] for i in range(seq_count // SEG)]
    blocks = lax.all_to_all(payload, "seq", 0, 0, axis_index_groups=quads)
    folded = kernel(chain_fold_body, [(blocks.shape[1:], BF16)], "chain_fold")(blocks)
    later = [
        lax.ppermute(
            folded, "seq",
            [(i, i - SEG * s) for i in range(seq_count) if i % per_doc >= SEG * s],
        )
        for s in range(1, SEGS)
    ]
    walked = kernel(chain_walk_body, [((SEG, HD * heads // SEG, HD), BF16)], "chain_walk")(*later, blocks)
    adjoint = lax.all_to_all(walked, "seq", 0, 0, axis_index_groups=quads).reshape(heads, HD, HD)
    gdn_dq, gdn_dk, gdn_dv, gdn_dbeta, gdn_dgate = kernel(
        bind(gdn_post_body, heads=heads),
        [((toks, width), BF16)] * 3 + [((heads, toks), F32)] * 2,
        "gdn_post", flops=5 * 10**9,
    )(gdn_q, gdn_k, gdn_v, gdn_beta, gdn_gate, gdn_state[0], inverse, gdn_dout, adjoint)

    dout_keep, dout_send = kernel(
        att_dout_body, [((toks, PAIR), BF16)] * 2, "att_dout", flops=10**9
    )(*att_parts, att_out_w)
    dout_got = lax.ppermute(dout_send, "seq", swap)
    qd = [kernel(join_dout_body, [((2, PAIR, PAIR), BF16)], "att_join_dout")(q_pair, dout_keep, dout_got)]
    for _ in range(RING):
        qd.append(lax.ppermute(qd[-1], "seq", back))
    dq_pair, stats = kernel(
        att_rows_body, [((PAIR, PAIR), BF16), ((8, PAIR), F32)], "att_rows", flops=3 * 10**9
    )(qd[0], *kv)
    all_stats = [stats] + [
        lax.ppermute(
            stats, "seq",
            [(i, i - 2 * s) for i in range(seq_count) if i % per_doc >= 2 * s],
        )
        for s in range(RING, 0, -1)
    ][::-1]
    keep, send = kernel(
        att_cols_body, [((3, toks, PAIR), BF16)] * 2, "att_cols", flops=3 * 10**9,
        scratch=[pltpu.VMEM((3, PAIR, PAIR), BF16)],
    )(kv_pair, dq_pair, *qd, *all_stats)
    got = lax.ppermute(send, "seq", swap)
    att_dq, att_dk, att_dv = kernel(finish_body, [((toks, width), BF16)] * 3, "att_finish")(keep, got)
    return (att_dq, att_dk, att_dv, gdn_dq, gdn_dk, gdn_dv, gdn_dbeta, gdn_dgate)


def solution(mesh):
    tokens = P("seq", "head")
    rates = P("head", "seq")
    weight = P("head", None)
    return jax.shard_map(
        shards,
        mesh=mesh,
        in_specs=(
            tokens, tokens, tokens, tokens, weight,
            tokens, tokens, tokens, rates, rates, P("seq", "head", None, None), tokens, weight,
        ),
        out_specs=(tokens, tokens, tokens, tokens, tokens, tokens, rates, rates),
        check_vma=False,
    )
```
